32 devices in a mesh: groups: 2 (over x), energy: 8 (over z, y), space: 2 (over core).
Axes of the slice: x: 2, y: 2, z: 4, core: 2. Of those that a mesh axis runs over, the one named last changes fastest.
Arguments:
- ham_diag: float32 [2, 2, 512, 256], P('space', None, 'groups'), parts along dimension 2, as said below
- ham_coupling: float32 [2, 2, 256, 256], P('groups'), parts along dimension 0, may hold values from -0.25 to 0.25
- sigma_shift: float32 [8, 2, 512], P('energy', 'space', 'groups'), parts along dimension 2, may hold values from -3 to 3
- sigma_width: float32 [8, 2, 512], P('energy', 'space', 'groups'), parts along dimension 2, may hold values from 0.5 to 2
- occupation: float32 [8, 2, 512], P('energy', 'space', 'groups'), parts along dimension 2, may hold values from 0 to 1
Outputs:
- polarization: float32 [16, 2, 2, 256, 256], P('groups', None, None, ('energy', 'space')), parts along dimension 0
The draws below stay inside these ranges and needn't reach their ends.
There are 2 independent parts, one for each index of `groups`. The reference program is written for one: setup_inputs(seed, part) draws one part's arguments, and reference() takes and returns one part's arrays. A program takes and returns all parts, laid end to end along the dimension named above; each array names one. Nothing has to cross between parts.
Inputs may be any that keep to these rules, and one draw needn't show every extreme that they name: Each ham_diag[b, 0] is symmetric and each ham_diag[b, 1] antisymmetric.
All inputs are finite; a program needn't handle non-finite values.
Results may differ from the reference program's by a relative error of at most 0.0001.
Values sent between devices are 32-bit elements; how exact they have to be, the bound alone decides.
A program may use at most 64 MiB of HBM per device.

```python
import math
import jax
import jax.numpy as jnp
from jax import lax

NORB = 256
NBLK = 2
NE = 8


def draw_ham_diag(key, part):
    first_key, second_key = jax.random.split(key)
    first = jax.random.truncated_normal(first_key, -3.0, 3.0, (NBLK, NORB, NORB), jnp.float32)
    second = jax.random.truncated_normal(second_key, -3.0, 3.0, (NBLK, NORB, NORB), jnp.float32)
    factor = 0.5 / NORB ** 0.5
    real_part = (first + jnp.swapaxes(first, 1, 2)) * factor
    imag_part = (second - jnp.swapaxes(second, 1, 2)) * factor
    return jnp.stack([real_part, imag_part], axis=1).astype(jnp.float32)


def levels(rng, dims, shards, low, largest):
    factor_of, own = 1.0, jax.random.fold_in(rng, 6)
    for dim, blocks in shards:
        steps = jnp.exp(jax.random.uniform(jax.random.fold_in(own, dim), (blocks,), jnp.float32, low / len(shards), largest / len(shards)))
        factor_of = factor_of * jnp.repeat(steps, dims[dim] // blocks).reshape([-1 if axis == dim else 1 for axis in range(len(dims))])
    return factor_of


def normal_values(stream_key, dims, width, reach, shards=(), kind=jnp.bfloat16):
    level = levels(stream_key, dims, shards, -0.22, 0.18) if shards else 1.0
    entries = jax.random.normal(stream_key, dims, jnp.float32) * width * level
    return jnp.minimum(jnp.maximum(entries, -reach), reach).astype(kind)


def setup_inputs(seed: int = 0, part: int = 0) -> dict:
    key_list = jax.random.split(jax.random.key(seed), 6)
    part_keys = jax.random.split(jax.random.fold_in(key_list[5], part), 6)
    ham_diag = draw_ham_diag(jax.random.fold_in(jax.random.fold_in(key_list[5], part), 71), part)
    ham_coupling = normal_values(part_keys[1], (NBLK - 1, 2, NORB, NORB), (2 * NORB) ** -0.5, 0.25, (), jnp.float32)
    sigma_shift = normal_values(part_keys[2], (NE, NBLK, NORB), 0.5, 3.0, ((0, 8), (1, 2)), jnp.float32)
    sigma_width = jnp.clip(jnp.exp(math.log(2.0) - 1.3862944 * jax.random.uniform(part_keys[3], (NE, NBLK, NORB), jnp.float32) ** levels(part_keys[3], (NE, NBLK, NORB), ((0, 8), (1, 2)), -0.2, 0.2)), 0.5, 2.0)
    occupation = jnp.clip(1.0 * jax.random.uniform(part_keys[4], (NE, NBLK, NORB), jnp.float32) ** levels(part_keys[4], (NE, NBLK, NORB), ((0, 8), (1, 2)), -0.2, 0.2), 0.0, 1.0)
    return {"ham_diag": ham_diag, "ham_coupling": ham_coupling, "sigma_shift": sigma_shift, "sigma_width": sigma_width, "occupation": occupation}


def matmul(left, right):
    return jnp.einsum('...ij,...jk->...ik', left, right, precision=lax.Precision.HIGHEST)

def cmul(left, right):
    left_re, left_im = (left[..., 0, :, :], left[..., 1, :, :])
    right_re, right_im = (right[..., 0, :, :], right[..., 1, :, :])
    return jnp.stack([matmul(left_re, right_re) - matmul(left_im, right_im), matmul(left_re, right_im) + matmul(left_im, right_re)], axis=-3)

def adjoint(value):
    return jnp.stack([jnp.swapaxes(value[..., 0, :, :], -1, -2), -jnp.swapaxes(value[..., 1, :, :], -1, -2)], axis=-3)

def invert(value):
    real_part = value[..., 0, :, :]
    imag_part = value[..., 1, :, :]
    normal = cmul(adjoint(value), value)
    upper = jnp.concatenate([normal[..., 0, :, :], -normal[..., 1, :, :]], axis=-1)
    lower = jnp.concatenate([normal[..., 1, :, :], normal[..., 0, :, :]], axis=-1)
    factor = jnp.linalg.cholesky(jnp.concatenate([upper, lower], axis=-2))
    target = jnp.concatenate([jnp.swapaxes(real_part, -1, -2), -jnp.swapaxes(imag_part, -1, -2)], axis=-2)
    middle = lax.linalg.triangular_solve(factor, target, left_side=True, lower=True)
    solved = lax.linalg.triangular_solve(factor, middle, left_side=True, lower=True, transpose_a=True)
    order = real_part.shape[-1]
    return jnp.stack([solved[..., :order, :], solved[..., order:, :]], axis=-3)

def sandwich(outer, inner):
    return cmul(cmul(outer, inner), adjoint(outer))

def add_imag_diagonal(matrix, values):
    identity = jnp.eye(values.shape[-1], dtype=jnp.float32)
    extra = jnp.stack([jnp.zeros_like(matrix[..., 0, :, :]), values[..., :, None] * identity], axis=-3)
    return matrix + extra

def reference(ham_diag, ham_coupling, sigma_shift, sigma_width, occupation):
    order = ham_diag.shape[-1]
    energy = -2.0 + 4.0 * (jnp.arange(NE).astype(jnp.float32) + 0.5) / NE
    identity = jnp.eye(order, dtype=jnp.float32)
    real_part = energy[:, None, None, None] * identity - ham_diag[None, :, 0] - sigma_shift[..., :, None] * identity
    imag_part = sigma_width[..., :, None] * identity - ham_diag[None, :, 1]
    system = jnp.stack([real_part, imag_part], axis=2)
    source = 2.0 * occupation * sigma_width
    left_sig = []
    left_less = []
    for block in range(NBLK):
        diagonal = system[:, block]
        if block == 0:
            coupled = jnp.zeros_like(diagonal)
            coupled_less = jnp.zeros_like(diagonal)
        else:
            link = adjoint(ham_coupling[block - 1])
            coupled = sandwich(link, green)
            coupled_less = sandwich(link, green_less)
        green = invert(diagonal - coupled)
        green_less = sandwich(green, add_imag_diagonal(coupled_less, source[:, block]))
        left_sig.append(coupled)
        left_less.append(coupled_less)
    right_sig = [None] * NBLK
    right_less = [None] * NBLK
    for block in reversed(range(NBLK)):
        diagonal = system[:, block]
        if block == NBLK - 1:
            coupled = jnp.zeros_like(diagonal)
            coupled_less = jnp.zeros_like(diagonal)
        else:
            link = ham_coupling[block]
            coupled = sandwich(link, rgreen)
            coupled_less = sandwich(link, rgreen_less)
        rgreen = invert(diagonal - coupled)
        rgreen_less = sandwich(rgreen, add_imag_diagonal(coupled_less, source[:, block]))
        right_sig[block] = coupled
        right_less[block] = coupled_less
    retarded = []
    lesser = []
    for block in range(NBLK):
        diagonal = system[:, block]
        full = invert(diagonal - left_sig[block] - right_sig[block])
        full_less = sandwich(full, add_imag_diagonal(left_less[block] + right_less[block], source[:, block]))
        retarded.append(full)
        lesser.append(full_less)
    retarded = jnp.stack(retarded, axis=1)
    lesser = jnp.stack(lesser, axis=1)
    greater = lesser + retarded - adjoint(retarded)
    a_re, a_im = (lesser[:, :, 0], lesser[:, :, 1])
    b_re, b_im = (greater[:, :, 0], greater[:, :, 1])
    corr_re = []
    corr_im = []
    for shift in range(NE):
        upper_re, upper_im = (a_re[shift:], a_im[shift:])
        lower_re, lower_im = (b_re[:NE - shift], b_im[:NE - shift])
        corr_re.append(jnp.sum(upper_re * lower_re + upper_im * lower_im, axis=0))
        corr_im.append(jnp.sum(upper_im * lower_re - upper_re * lower_im, axis=0))
    corr_re = jnp.stack(corr_re, axis=0)
    corr_im = jnp.stack(corr_im, axis=0)
    return jnp.stack([-order * corr_im, order * corr_re], axis=2)
```

```python
import functools

import jax
import jax.numpy as jnp
from jax import lax
from jax.experimental import pallas as pl
from jax.experimental.pallas import tpu as pltpu
from jax.sharding import PartitionSpec as P

F32 = jnp.float32
BF16 = jnp.bfloat16
NN = (((1,), (0,)), ((), ()))
NT = (((1,), (1,)), ((), ()))


def embed(right):
    half = right.shape[1] // 2
    return jnp.concatenate(
        [right, jnp.concatenate([-right[:, half:], right[:, :half]], axis=1)], axis=0
    )


def split(value):
    high = value.astype(BF16)
    return high, (value - high.astype(F32)).astype(BF16)


def dot(left, right, dims):
    return lax.dot_general(left, right, dims, preferred_element_type=F32)


def mul1(left, right, dims=NN):
    return dot(left.astype(BF16), embed(right.astype(BF16)), dims)


def mul3(left, right, dims=NN):
    left_hi, left_lo = split(left)
    right_hi, right_lo = split(right)
    wide = embed(right_hi)
    return dot(left_hi, wide, dims) + dot(left_lo, wide, dims) + dot(left_hi, embed(right_lo), dims)


def adjoint(value):
    half = value.shape[1] // 2
    return jnp.concatenate([value[:, :half].T, -value[:, half:].T], axis=1)


def eye2(order):
    row = lax.broadcasted_iota(jnp.int32, (order, 2 * order), 0)
    col = lax.broadcasted_iota(jnp.int32, (order, 2 * order), 1)
    return jnp.where(row == col, 1.0, 0.0).astype(F32)


def total(value):
    return jnp.sum(value * value)


def invert(a_ref, ah_ref, pair_ref, floor):
    order = a_ref.shape[0]
    normal = mul1(a_ref[...], a_ref[...], NT)
    bound = jnp.sqrt(total(normal))
    pair_ref[:order, :] = ah_ref[...] / bound
    pair_ref[order:, :] = normal / bound

    def rough(low):
        scale = 2.0 / (1.0 + low)
        pair = pair_ref[...]
        pair_ref[...] = (2.0 * scale) * pair - (scale * scale) * mul1(pair, pair_ref[order:, :])
        rho = (1.0 - low) / (1.0 + low)
        return 1.0 - rho * rho

    lax.while_loop(lambda low: low < 0.9, rough, jnp.maximum(floor / bound, 1e-6))

    def residual():
        return eye2(order) - mul3(a_ref[...], pair_ref[:order, :])

    def refine(state):
        step, _ = state
        left = residual()
        inverse = pair_ref[:order, :]
        pair_ref[:order, :] = inverse + mul1(inverse, left)
        return step + 1, total(left)

    _, size = lax.while_loop(
        lambda s: (s[0] < 5) & (s[1] > 4e-6), refine, (jnp.int32(0), F32(1.0))
    )

    @pl.when(jnp.logical_not(size <= 4e-6))
    def _():
        pair_ref[:order, :] = ah_ref[...] / bound

        def careful(state):
            step, _ = state
            left = residual()
            inverse = pair_ref[:order, :]
            pair_ref[:order, :] = inverse + mul3(inverse, left)
            return step + 1, total(left)

        lax.while_loop(
            lambda s: (s[0] < 60) & (s[1] > 4e-6), careful, (jnp.int32(0), F32(1.0))
        )


def green_kernel(scal_ref, side_ref, link_ref, far_ref, near_ref, sfar_ref, snear_ref, out_ref,
                 a_ref, ah_ref, pair_ref, x_ref):
    order = far_ref.shape[-1]
    energy = scal_ref[0]
    row = lax.broadcasted_iota(jnp.int32, (order, order), 0)
    col = lax.broadcasted_iota(jnp.int32, (order, order), 1)
    on = row == col

    def system(ham_ref, sig_ref):
        real = jnp.where(on, energy - sig_ref[0:1, :], 0.0) - ham_ref[0]
        width = jnp.where(on, sig_ref[1:2, :], 0.0)
        imag = width - ham_ref[1]
        return (jnp.concatenate([real, imag], axis=1),
                jnp.concatenate([real, -width - ham_ref[1]], axis=1))

    a_ref[...], ah_ref[...] = system(far_ref, sfar_ref)
    floor = jnp.min(sfar_ref[1:2, :])
    invert(a_ref, ah_ref, pair_ref, floor * floor)

    link = jnp.concatenate([link_ref[0], link_ref[1]], axis=1)
    link = jnp.where(side_ref[0] == 0, link, adjoint(link))
    x_ref[...] = mul3(link, pair_ref[:order, :])
    coupled = mul3(x_ref[...], link, NT)
    own, own_h = system(near_ref, snear_ref)
    a_ref[...] = own - coupled
    ah_ref[...] = own_h - adjoint(coupled)
    floor = jnp.min(snear_ref[1:2, :])
    invert(a_ref, ah_ref, pair_ref, floor * floor)

    green = pair_ref[:order, :]
    mixed = mul3(green, x_ref[...])

    def source(sig_ref):
        value = 2.0 * sig_ref[2:3, :] * sig_ref[1:2, :]
        return jnp.concatenate([value, value], axis=1)

    less = mul3(green * source(snear_ref), green, NT) + mul3(mixed * source(sfar_ref), mixed, NT)
    k_re, k_im = -less[:, order:], less[:, :order]
    g_re, g_im = green[:, :order], green[:, order:]
    out_ref[:, :order] = k_re
    out_ref[:, order:2 * order] = k_im
    out_ref[:, 2 * order:3 * order] = k_re + g_re - g_re.T
    out_ref[:, 3 * order:] = k_im + g_im + g_im.T


VMEM = pl.BlockSpec(memory_space=pltpu.VMEM)
SMEM = pl.BlockSpec(memory_space=pltpu.SMEM)


def green_blocks(energy, side, link, far, near, sfar, snear):
    order = far.shape[-1]
    return pl.pallas_call(
        green_kernel,
        out_shape=jax.ShapeDtypeStruct((order, 4 * order), F32),
        in_specs=[SMEM, SMEM, VMEM, VMEM, VMEM, VMEM, VMEM],
        out_specs=VMEM,
        scratch_shapes=[
            pltpu.VMEM((order, 2 * order), F32),
            pltpu.VMEM((order, 2 * order), F32),
            pltpu.VMEM((2 * order, 2 * order), F32),
            pltpu.VMEM((order, 2 * order), F32),
        ],
        compiler_params=pltpu.CompilerParams(vmem_limit_bytes=48 * 2**20),
    )(energy, side, link, far, near, sfar, snear)


def body(ham_diag, ham_coupling, sigma_shift, sigma_width, occupation):
    order = ham_diag.shape[-1]
    count = lax.axis_size("energy")
    sides = lax.axis_size("space")
    side = lax.axis_index("space")
    energy = -2.0 + 4.0 * (lax.axis_index("energy").astype(F32) + 0.5) / count
    near = ham_diag[0]
    snear = jnp.concatenate([sigma_shift[0], sigma_width[0], occupation[0]], axis=0)
    swap = [(0, 1), (1, 0)]
    far, sfar = lax.ppermute((near, snear), "space", swap)
    mine = green_blocks(energy.reshape(1), side.reshape(1), ham_coupling[0], far, near, sfar, snear)
    arrived = lax.all_to_all(mine, ("energy", "space"), split_axis=0, concat_axis=0, tiled=True)
    rows = order // (count * sides)
    arrived = arrived.reshape(count, sides, rows, 4, order)
    k_re, k_im, q_re, q_im = (arrived[:, :, :, i] for i in range(4))
    out = []
    for k in range(count):
        kr, ki = k_re[k:], k_im[k:]
        qr, qi = q_re[:count - k], q_im[:count - k]
        corr_re = jnp.sum(kr * qr + ki * qi, axis=0)
        corr_im = jnp.sum(ki * qr - kr * qi, axis=0)
        out.append(jnp.stack([-order * corr_im, order * corr_re], axis=1))
    return jnp.stack(out, axis=0)


def solution(mesh):
    return jax.shard_map(
        body,
        mesh=mesh,
        in_specs=(
            P("space", None, "groups", None),
            P("groups", None, None, None),
            P("energy", "space", "groups"),
            P("energy", "space", "groups"),
            P("energy", "space", "groups"),
        ),
        out_specs=P("groups", None, None, ("energy", "space"), None),
        check_vma=False,
    )
```

```python
import functools

import jax
import jax.numpy as jnp
from jax import lax
from jax.experimental import pallas as pl
from jax.experimental.pallas import tpu as pltpu
from jax.sharding import PartitionSpec as P

F32 = jnp.float32
BF16 = jnp.bfloat16
NN = (((1,), (0,)), ((), ()))
NT = (((1,), (1,)), ((), ()))


def embed(right):
    half = right.shape[1] // 2
    return jnp.concatenate(
        [right, jnp.concatenate([-right[:, half:], right[:, :half]], axis=1)], axis=0
    )


def split(value):
    high = value.astype(BF16)
    return high, (value - high.astype(F32)).astype(BF16)


def dot(left, right, dims):
    return lax.dot_general(left, right, dims, preferred_element_type=F32)


def mul1(left, right, dims=NN):
    return dot(left.astype(BF16), embed(right.astype(BF16)), dims)


def mul3(left, right, dims=NN):
    left_hi, left_lo = split(left)
    right_hi, right_lo = split(right)
    wide = embed(right_hi)
    return dot(left_hi, wide, dims) + dot(left_lo, wide, dims) + dot(left_hi, embed(right_lo), dims)


def adjoint(value):
    half = value.shape[1] // 2
    return jnp.concatenate([value[:, :half].T, -value[:, half:].T], axis=1)


def eye2(order):
    row = lax.broadcasted_iota(jnp.int32, (order, 2 * order), 0)
    col = lax.broadcasted_iota(jnp.int32, (order, 2 * order), 1)
    return jnp.where(row == col, 1.0, 0.0).astype(F32)


def total(value):
    return jnp.sum(value * value)


def invert(a_ref, ah_ref, pair_ref, floors):
    batch, order = a_ref.shape[:2]
    each = range(batch)
    bounds = []
    for j in each:
        normal = mul1(a_ref[j], a_ref[j], NT)
        bounds.append(jnp.sqrt(total(normal)))
        pair_ref[j, :order] = ah_ref[j] / bounds[j]
        pair_ref[j, order:] = normal / bounds[j]

    def rough(lows):
        after = []
        for j in each:
            low = lows[j]
            scale = 2.0 / (1.0 + low)
            pair = pair_ref[j]
            pair_ref[j] = (2.0 * scale) * pair - (scale * scale) * mul1(pair, pair[order:])
            rho = (1.0 - low) / (1.0 + low)
            after.append(1.0 - rho * rho)
        return tuple(after)

    lowest = lambda lows: functools.reduce(jnp.minimum, lows)
    largest = lambda sizes: functools.reduce(jnp.maximum, sizes)
    lax.while_loop(
        lambda lows: lowest(lows) < 0.9,
        rough,
        tuple(jnp.maximum(floors[j] / bounds[j], 1e-6) for j in each),
    )

    def newton(mul):
        def step(state):
            sizes = []
            for j in each:
                inverse = pair_ref[j, :order]
                left = eye2(order) - mul3(a_ref[j], inverse)
                pair_ref[j, :order] = inverse + mul(inverse, left)
                sizes.append(total(left))
            return state[0] + 1, largest(sizes)

        return step

    def iterate(mul, limit):
        return lax.while_loop(
            lambda s: (s[0] < limit) & (s[1] > 4e-6), newton(mul), (jnp.int32(0), F32(1.0))
        )[1]

    size = iterate(mul1, 5)

    @pl.when(jnp.logical_not(size <= 4e-6))
    def _():
        for j in each:
            pair_ref[j, :order] = ah_ref[j] / bounds[j]
        iterate(mul3, 60)


def green_kernel(scal_ref, side_ref, link_ref, far_ref, near_ref, sig_ref, green_ref, x_ref,
                 a_ref, ah_ref, pair_ref):
    order = far_ref.shape[-1]
    batch = sig_ref.shape[0]
    row = lax.broadcasted_iota(jnp.int32, (order, order), 0)
    col = lax.broadcasted_iota(jnp.int32, (order, order), 1)
    on = row == col

    def system(ham_ref, j, which):
        real = jnp.where(on, scal_ref[j] - sig_ref[j, which, 0:1, :], 0.0) - ham_ref[0]
        width = jnp.where(on, sig_ref[j, which, 1:2, :], 0.0)
        return (jnp.concatenate([real, width - ham_ref[1]], axis=1),
                jnp.concatenate([real, -width - ham_ref[1]], axis=1))

    def floors(which):
        least = [jnp.min(sig_ref[j, which, 1:2, :]) for j in range(batch)]
        return [value * value for value in least]

    for j in range(batch):
        a_ref[j], ah_ref[j] = system(far_ref, j, 1)
    invert(a_ref, ah_ref, pair_ref, floors(1))
    link = jnp.concatenate([link_ref[0], link_ref[1]], axis=1)
    link = jnp.where(side_ref[0] == 0, link, adjoint(link))
    for j in range(batch):
        x_ref[j] = mul3(link, pair_ref[j, :order])
        coupled = mul3(x_ref[j], link, NT)
        own, own_h = system(near_ref, j, 0)
        a_ref[j] = own - coupled
        ah_ref[j] = own_h - adjoint(coupled)
    invert(a_ref, ah_ref, pair_ref, floors(0))
    for j in range(batch):
        green_ref[j] = pair_ref[j, :order]


def lesser_greater(green, mixed, adj, near, far, g_rows, m_rows):
    order = green.shape[0]

    def source(sig):
        value = 2.0 * sig[2:3, :] * sig[1:2, :]
        return jnp.concatenate([value, value], axis=1)

    less = mul3(g_rows * source(near), green, NT) + mul3(m_rows * source(far), mixed, NT)
    k = jnp.concatenate([-less[:, order:], less[:, :order]], axis=1)
    return jnp.concatenate([k, k + g_rows - adj], axis=1)


def local_kernel(sig_ref, green_ref, x_ref, out_ref):
    green = green_ref[0]
    mixed = mul3(green, x_ref[0])
    out_ref[...] = lesser_greater(
        green, mixed, adjoint(green), sig_ref[0, 0], sig_ref[0, 1], green, mixed
    )


def exchange_kernel(sig_ref, green_ref, x_ref, out_ref, mix_ref, adj_ref, send_ref, recv_ref,
                    send_sem, recv_sem):
    peers, batch, rows = recv_ref.shape[:3]
    span = peers * rows
    order = green_ref.shape[1]
    spaces = lax.axis_size("space")
    per_side = peers // spaces
    where = lax.axis_index("energy")
    half = where // per_side
    me = (where - half * per_side) * spaces + lax.axis_index("space")

    def device(peer):
        return {"energy": half * per_side + peer // spaces, "space": peer % spaces}

    barrier = pltpu.get_barrier_semaphore()
    for hop in range(1, peers):
        pl.semaphore_signal(barrier, inc=1, device_id=device(me ^ hop),
                            device_id_type=pl.DeviceIdType.MESH)
    here = pl.ds(pl.multiple_of(half * span, span), span)
    copies = []
    for j in range(batch):
        mix_ref[...] = mul3(green_ref[j], x_ref[j])
        adj_ref[...] = adjoint(green_ref[j])
        send_ref[j] = lesser_greater(
            green_ref[j], mix_ref[...], adj_ref[here], sig_ref[j, 0], sig_ref[j, 1],
            green_ref[j, here], mix_ref[here],
        )
        if j == 0:
            pl.semaphore_wait(barrier, peers - 1)
        for hop in reversed(range(1, peers)):
            peer = me ^ hop
            copy = pltpu.make_async_remote_copy(
                src_ref=send_ref.at[j, pl.ds(pl.multiple_of(peer * rows, rows), rows)],
                dst_ref=recv_ref.at[me, j],
                send_sem=send_sem.at[j, hop],
                recv_sem=recv_sem.at[j, hop],
                device_id=device(peer),
                device_id_type=pl.DeviceIdType.MESH,
            )
            copy.start()
            copies.append(copy)
        recv_ref[me, j] = send_ref[j, pl.ds(pl.multiple_of(me * rows, rows), rows)]
    for copy in copies:
        copy.wait()
    count = per_side * batch
    for s in range(spaces):
        def part(n, i):
            return recv_ref[n % per_side * spaces + s, n // per_side, :, i * order:(i + 1) * order]

        for k in range(count):
            corr_re = jnp.zeros((rows, order), F32)
            corr_im = jnp.zeros((rows, order), F32)
            for n in range(k, count):
                kr, ki, qr, qi = part(n, 0), part(n, 1), part(n - k, 2), part(n - k, 3)
                corr_re += kr * qr + ki * qi
                corr_im += ki * qr - kr * qi
            out_ref[k, s, 0] = -order * corr_im
            out_ref[k, s, 1] = order * corr_re


VMEM = pl.BlockSpec(memory_space=pltpu.VMEM)
SMEM = pl.BlockSpec(memory_space=pltpu.SMEM)
LIMIT = 48 * 2**20


def green_blocks(energy, side, link, far, near, sig):
    order = far.shape[-1]
    batch = sig.shape[0]
    shape = (batch, order, 2 * order)
    return pl.pallas_call(
        green_kernel,
        out_shape=[jax.ShapeDtypeStruct(shape, F32)] * 2,
        in_specs=[SMEM, SMEM, VMEM, VMEM, VMEM, VMEM],
        out_specs=[VMEM, VMEM],
        scratch_shapes=[
            pltpu.VMEM(shape, F32),
            pltpu.VMEM(shape, F32),
            pltpu.VMEM((batch, 2 * order, 2 * order), F32),
        ],
        compiler_params=pltpu.CompilerParams(vmem_limit_bytes=LIMIT),
    )(energy, side, link, far, near, sig)


def exchange(sig, green, x, peers, rows):
    batch, order = green.shape[:2]
    spaces = lax.axis_size("space")
    return pl.pallas_call(
        exchange_kernel,
        out_shape=jax.ShapeDtypeStruct((peers // spaces * batch, spaces, 2, rows, order), F32),
        in_specs=[VMEM, VMEM, VMEM],
        out_specs=VMEM,
        scratch_shapes=[
            pltpu.VMEM((order, 2 * order), F32),
            pltpu.VMEM((order, 2 * order), F32),
            pltpu.VMEM((batch, peers * rows, 4 * order), F32),
            pltpu.VMEM((peers, batch, rows, 4 * order), F32),
            pltpu.SemaphoreType.DMA((batch, peers)),
            pltpu.SemaphoreType.DMA((batch, peers)),
        ],
        compiler_params=pltpu.CompilerParams(
            vmem_limit_bytes=LIMIT, collective_id=0, has_side_effects=True
        ),
    )(sig, green, x)


def collect(mine, count, sides, rows):
    order = mine.shape[0]
    arrived = lax.all_to_all(mine, ("energy", "space"), split_axis=0, concat_axis=0, tiled=True)
    arrived = arrived.reshape(count, sides, rows, 4, order)
    k_re, k_im, q_re, q_im = (arrived[:, :, :, i] for i in range(4))
    out = []
    for k in range(count):
        kr, ki = k_re[k:], k_im[k:]
        qr, qi = q_re[:count - k], q_im[:count - k]
        corr_re = jnp.sum(kr * qr + ki * qi, axis=0)
        corr_im = jnp.sum(ki * qr - kr * qi, axis=0)
        out.append(jnp.stack([-order * corr_im, order * corr_re], axis=1))
    return jnp.stack(out, axis=0)


SIDES = 2


def body(ham_diag, ham_coupling, sigma_shift, sigma_width, occupation):
    order = ham_diag.shape[-1]
    count = lax.axis_size("energy")
    spaces = lax.axis_size("space")
    side = lax.axis_index("space")
    where = lax.axis_index("energy")
    rows = order // (count * spaces)
    direct = rows % 8 == 0 and count & (count - 1) == 0
    batch = SIDES if direct and count % SIDES == 0 else 1
    per_side = count // batch
    near = ham_diag[0]
    far = lax.ppermute(near, "space", [(0, 1), (1, 0)])
    packed = jnp.concatenate([sigma_shift[0], sigma_width[0], occupation[0]], axis=0)
    sig = []
    for j in range(batch):
        pair = []
        for flip in range(spaces):
            moves = [(e * spaces + s, (e + j * per_side) % count * spaces + (s ^ flip))
                     for e in range(count) for s in range(spaces)]
            pair.append(packed if j == flip == 0 else lax.ppermute(packed, ("energy", "space"), moves))
        sig.append(jnp.stack(pair))
    index = (where + per_side * jnp.arange(batch)) % count
    energy = -2.0 + 4.0 * (index.astype(F32) + 0.5) / count
    sig = jnp.stack(sig)
    if batch > 1:
        flip = where >= per_side
        sig = jnp.where(flip, sig[::-1], sig)
        energy = jnp.where(flip, energy[::-1], energy)
    green, x = green_blocks(energy, side.reshape(1), ham_coupling[0], far, near, sig)
    if direct:
        return exchange(sig, green, x, per_side * spaces, rows)
    mine = pl.pallas_call(
        local_kernel,
        out_shape=jax.ShapeDtypeStruct((order, 4 * order), F32),
        in_specs=[VMEM, VMEM, VMEM],
        out_specs=VMEM,
        compiler_params=pltpu.CompilerParams(vmem_limit_bytes=LIMIT),
    )(sig, green, x)
    return collect(mine, count, spaces, rows)


def solution(mesh):
    return jax.shard_map(
        body,
        mesh=mesh,
        in_specs=(
            P("space", None, "groups", None),
            P("groups", None, None, None),
            P("energy", "space", "groups"),
            P("energy", "space", "groups"),
            P("energy", "space", "groups"),
        ),
        out_specs=P("groups", None, None, ("energy", "space"), None),
        check_vma=False,
    )
```

```python
import functools

import jax
import jax.numpy as jnp
from jax import lax
from jax.experimental import pallas as pl
from jax.experimental.pallas import tpu as pltpu
from jax.sharding import PartitionSpec as P

F32 = jnp.float32
BF16 = jnp.bfloat16
NN = (((1,), (0,)), ((), ()))
NT = (((1,), (1,)), ((), ()))


def split(value):
    high = value.astype(BF16)
    return high, (value - high.astype(F32)).astype(BF16)


def dot(left, right, dims):
    return lax.dot_general(left, right, dims, preferred_element_type=F32)


def three_products(left, right, dims, real_dot):
    half = left.shape[1] // 2
    left_re, left_im = left[:, :half], left[:, half:]
    right_re, right_im = right[:, :half], right[:, half:]
    first = real_dot(left_re, right_re, dims)
    second = real_dot(left_im, right_im, dims)
    if dims is NT:
        third = real_dot(left_re + left_im, right_re - right_im, dims)
        return jnp.concatenate([first + second, third - first + second], axis=1)
    third = real_dot(left_re + left_im, right_re + right_im, dims)
    return jnp.concatenate([first - second, third - first - second], axis=1)


def dot1(left, right, dims):
    return dot(left.astype(BF16), right.astype(BF16), dims)


def dot3(left, right, dims):
    left_hi, left_lo = split(left)
    right_hi, right_lo = split(right)
    return (dot(left_hi, right_hi, dims) + dot(left_lo, right_hi, dims)
            + dot(left_hi, right_lo, dims))


def mul1(left, right, dims=NN):
    return three_products(left, right, dims, dot1)


def mul3(left, right, dims=NN):
    return three_products(left, right, dims, dot3)


def adjoint(value):
    half = value.shape[1] // 2
    return jnp.concatenate([value[:, :half].T, -value[:, half:].T], axis=1)


def eye2(order):
    row = lax.broadcasted_iota(jnp.int32, (order, 2 * order), 0)
    col = lax.broadcasted_iota(jnp.int32, (order, 2 * order), 1)
    return jnp.where(row == col, 1.0, 0.0).astype(F32)


def total(value):
    return jnp.sum(value * value)


def invert(a_ref, ah_ref, pair_ref, floors):
    batch, order = a_ref.shape[:2]
    each = range(batch)
    bounds = []
    for j in each:
        normal = mul1(a_ref[j], a_ref[j], NT)
        bounds.append(jnp.sqrt(total(normal)))
        pair_ref[j, :order] = ah_ref[j] / bounds[j]
        pair_ref[j, order:] = normal / bounds[j]

    def rough(lows):
        after = []
        for j in each:
            low = lows[j]
            scale = 2.0 / (1.0 + low)
            pair = pair_ref[j]
            pair_ref[j] = (2.0 * scale) * pair - (scale * scale) * mul1(pair, pair[order:])
            rho = (1.0 - low) / (1.0 + low)
            after.append(1.0 - rho * rho)
        return tuple(after)

    lowest = lambda lows: functools.reduce(jnp.minimum, lows)
    largest = lambda sizes: functools.reduce(jnp.maximum, sizes)
    lax.while_loop(
        lambda lows: lowest(lows) < 0.9,
        rough,
        tuple(jnp.maximum(floors[j] / bounds[j], 1e-6) for j in each),
    )

    def newton(mul):
        def step(state):
            sizes = []
            for j in each:
                inverse = pair_ref[j, :order]
                left = eye2(order) - mul3(a_ref[j], inverse)
                pair_ref[j, :order] = inverse + mul(inverse, left)
                sizes.append(total(left))
            return state[0] + 1, largest(sizes)

        return step

    def iterate(mul, limit):
        return lax.while_loop(
            lambda s: (s[0] < limit) & (s[1] > 4e-6), newton(mul), (jnp.int32(0), F32(1.0))
        )[1]

    size = iterate(mul1, 5)

    @pl.when(jnp.logical_not(size <= 4e-6))
    def _():
        for j in each:
            pair_ref[j, :order] = ah_ref[j] / bounds[j]
        iterate(mul3, 60)


def green_kernel(scal_ref, side_ref, link_ref, far_ref, near_ref, sig_ref, green_ref, x_ref,
                 a_ref, ah_ref, pair_ref):
    order = far_ref.shape[-1]
    batch = sig_ref.shape[0]
    row = lax.broadcasted_iota(jnp.int32, (order, order), 0)
    col = lax.broadcasted_iota(jnp.int32, (order, order), 1)
    on = row == col

    def system(ham_ref, j, which):
        real = jnp.where(on, scal_ref[j] - sig_ref[j, which, 0:1, :], 0.0) - ham_ref[0]
        width = jnp.where(on, sig_ref[j, which, 1:2, :], 0.0)
        return (jnp.concatenate([real, width - ham_ref[1]], axis=1),
                jnp.concatenate([real, -width - ham_ref[1]], axis=1))

    def floors(which):
        least = [jnp.min(sig_ref[j, which, 1:2, :]) for j in range(batch)]
        return [value * value for value in least]

    for j in range(batch):
        a_ref[j], ah_ref[j] = system(far_ref, j, 1)
    invert(a_ref, ah_ref, pair_ref, floors(1))
    link = jnp.concatenate([link_ref[0], link_ref[1]], axis=1)
    link = jnp.where(side_ref[0] == 0, link, adjoint(link))
    for j in range(batch):
        x_ref[j] = mul3(link, pair_ref[j, :order])
        coupled = mul3(x_ref[j], link, NT)
        own, own_h = system(near_ref, j, 0)
        a_ref[j] = own - coupled
        ah_ref[j] = own_h - adjoint(coupled)
    invert(a_ref, ah_ref, pair_ref, floors(0))
    for j in range(batch):
        green_ref[j] = pair_ref[j, :order]


def lesser_greater(green, mixed, adj, near, far, g_rows, m_rows):
    order = green.shape[0]

    def source(sig):
        value = 2.0 * sig[2:3, :] * sig[1:2, :]
        return jnp.concatenate([value, value], axis=1)

    less = mul3(g_rows * source(near), green, NT) + mul3(m_rows * source(far), mixed, NT)
    k = jnp.concatenate([-less[:, order:], less[:, :order]], axis=1)
    return jnp.concatenate([k, k + g_rows - adj], axis=1)


def local_kernel(sig_ref, green_ref, x_ref, out_ref):
    green = green_ref[0]
    mixed = mul3(green, x_ref[0])
    out_ref[...] = lesser_greater(
        green, mixed, adjoint(green), sig_ref[0, 0], sig_ref[0, 1], green, mixed
    )


def exchange_kernel(sig_ref, green_ref, x_ref, out_ref, mix_ref, adj_ref, send_ref, recv_ref,
                    send_sem, recv_sem):
    peers, batch, rows = recv_ref.shape[:3]
    span = peers * rows
    order = green_ref.shape[1]
    spaces = lax.axis_size("space")
    per_side = peers // spaces
    where = lax.axis_index("energy")
    half = where // per_side
    me = (where - half * per_side) * spaces + lax.axis_index("space")

    def device(peer):
        return {"energy": half * per_side + peer // spaces, "space": peer % spaces}

    barrier = pltpu.get_barrier_semaphore()
    for hop in range(1, peers):
        pl.semaphore_signal(barrier, inc=1, device_id=device(me ^ hop),
                            device_id_type=pl.DeviceIdType.MESH)
    here = pl.ds(pl.multiple_of(half * span, span), span)
    copies = []
    for j in range(batch):
        mix_ref[...] = mul3(green_ref[j], x_ref[j])
        adj_ref[...] = adjoint(green_ref[j])
        send_ref[j] = lesser_greater(
            green_ref[j], mix_ref[...], adj_ref[here], sig_ref[j, 0], sig_ref[j, 1],
            green_ref[j, here], mix_ref[here],
        )
        if j == 0:
            pl.semaphore_wait(barrier, peers - 1)
        for hop in reversed(range(1, peers)):
            peer = me ^ hop
            copy = pltpu.make_async_remote_copy(
                src_ref=send_ref.at[j, pl.ds(pl.multiple_of(peer * rows, rows), rows)],
                dst_ref=recv_ref.at[me, j],
                send_sem=send_sem.at[j, hop],
                recv_sem=recv_sem.at[j, hop],
                device_id=device(peer),
                device_id_type=pl.DeviceIdType.MESH,
            )
            copy.start()
            copies.append(copy)
        recv_ref[me, j] = send_ref[j, pl.ds(pl.multiple_of(me * rows, rows), rows)]
    for copy in copies:
        copy.wait()
    count = per_side * batch
    for s in range(spaces):
        def part(n, i):
            return recv_ref[n % per_side * spaces + s, n // per_side, :, i * order:(i + 1) * order]

        for k in range(count):
            corr_re = jnp.zeros((rows, order), F32)
            corr_im = jnp.zeros((rows, order), F32)
            for n in range(k, count):
                kr, ki, qr, qi = part(n, 0), part(n, 1), part(n - k, 2), part(n - k, 3)
                corr_re += kr * qr + ki * qi
                corr_im += ki * qr - kr * qi
            out_ref[k, s, 0] = -order * corr_im
            out_ref[k, s, 1] = order * corr_re


VMEM = pl.BlockSpec(memory_space=pltpu.VMEM)
SMEM = pl.BlockSpec(memory_space=pltpu.SMEM)
LIMIT = 48 * 2**20


def green_blocks(energy, side, link, far, near, sig):
    order = far.shape[-1]
    batch = sig.shape[0]
    shape = (batch, order, 2 * order)
    return pl.pallas_call(
        green_kernel,
        out_shape=[jax.ShapeDtypeStruct(shape, F32)] * 2,
        in_specs=[SMEM, SMEM, VMEM, VMEM, VMEM, VMEM],
        out_specs=[VMEM, VMEM],
        scratch_shapes=[
            pltpu.VMEM(shape, F32),
            pltpu.VMEM(shape, F32),
            pltpu.VMEM((batch, 2 * order, 2 * order), F32),
        ],
        compiler_params=pltpu.CompilerParams(vmem_limit_bytes=LIMIT),
    )(energy, side, link, far, near, sig)


def exchange(sig, green, x, peers, rows):
    batch, order = green.shape[:2]
    spaces = lax.axis_size("space")
    return pl.pallas_call(
        exchange_kernel,
        out_shape=jax.ShapeDtypeStruct((peers // spaces * batch, spaces, 2, rows, order), F32),
        in_specs=[VMEM, VMEM, VMEM],
        out_specs=VMEM,
        scratch_shapes=[
            pltpu.VMEM((order, 2 * order), F32),
            pltpu.VMEM((order, 2 * order), F32),
            pltpu.VMEM((batch, peers * rows, 4 * order), F32),
            pltpu.VMEM((peers, batch, rows, 4 * order), F32),
            pltpu.SemaphoreType.DMA((batch, peers)),
            pltpu.SemaphoreType.DMA((batch, peers)),
        ],
        compiler_params=pltpu.CompilerParams(
            vmem_limit_bytes=LIMIT, collective_id=0, has_side_effects=True
        ),
    )(sig, green, x)


def collect(mine, count, sides, rows):
    order = mine.shape[0]
    arrived = lax.all_to_all(mine, ("energy", "space"), split_axis=0, concat_axis=0, tiled=True)
    arrived = arrived.reshape(count, sides, rows, 4, order)
    k_re, k_im, q_re, q_im = (arrived[:, :, :, i] for i in range(4))
    out = []
    for k in range(count):
        kr, ki = k_re[k:], k_im[k:]
        qr, qi = q_re[:count - k], q_im[:count - k]
        corr_re = jnp.sum(kr * qr + ki * qi, axis=0)
        corr_im = jnp.sum(ki * qr - kr * qi, axis=0)
        out.append(jnp.stack([-order * corr_im, order * corr_re], axis=1))
    return jnp.stack(out, axis=0)


SIDES = 1


def body(ham_diag, ham_coupling, sigma_shift, sigma_width, occupation):
    order = ham_diag.shape[-1]
    count = lax.axis_size("energy")
    spaces = lax.axis_size("space")
    side = lax.axis_index("space")
    where = lax.axis_index("energy")
    rows = order // (count * spaces)
    direct = rows % 8 == 0 and count & (count - 1) == 0
    batch = SIDES if direct and count % SIDES == 0 else 1
    per_side = count // batch
    near = ham_diag[0]
    far = lax.ppermute(near, "space", [(0, 1), (1, 0)])
    packed = jnp.concatenate([sigma_shift[0], sigma_width[0], occupation[0]], axis=0)
    sig = []
    for j in range(batch):
        pair = []
        for flip in range(spaces):
            moves = [(e * spaces + s, (e + j * per_side) % count * spaces + (s ^ flip))
                     for e in range(count) for s in range(spaces)]
            pair.append(packed if j == flip == 0 else lax.ppermute(packed, ("energy", "space"), moves))
        sig.append(jnp.stack(pair))
    index = (where + per_side * jnp.arange(batch)) % count
    energy = -2.0 + 4.0 * (index.astype(F32) + 0.5) / count
    sig = jnp.stack(sig)
    if batch > 1:
        flip = where >= per_side
        sig = jnp.where(flip, sig[::-1], sig)
        energy = jnp.where(flip, energy[::-1], energy)
    green, x = green_blocks(energy, side.reshape(1), ham_coupling[0], far, near, sig)
    if direct:
        return exchange(sig, green, x, per_side * spaces, rows)
    mine = pl.pallas_call(
        local_kernel,
        out_shape=jax.ShapeDtypeStruct((order, 4 * order), F32),
        in_specs=[VMEM, VMEM, VMEM],
        out_specs=VMEM,
        compiler_params=pltpu.CompilerParams(vmem_limit_bytes=LIMIT),
    )(sig, green, x)
    return collect(mine, count, spaces, rows)


def solution(mesh):
    return jax.shard_map(
        body,
        mesh=mesh,
        in_specs=(
            P("space", None, "groups", None),
            P("groups", None, None, None),
            P("energy", "space", "groups"),
            P("energy", "space", "groups"),
            P("energy", "space", "groups"),
        ),
        out_specs=P("groups", None, None, ("energy", "space"), None),
        check_vma=False,
    )
```

```python
import functools

import jax
import jax.numpy as jnp
from jax import lax
from jax.experimental import pallas as pl
from jax.experimental.pallas import tpu as pltpu
from jax.sharding import PartitionSpec as P

F32 = jnp.float32
BF16 = jnp.bfloat16
NN = (((1,), (0,)), ((), ()))
NT = (((1,), (1,)), ((), ()))


def split(value):
    high = value.astype(BF16)
    return high, (value - high.astype(F32)).astype(BF16)


def dot(left, right, dims):
    return lax.dot_general(left, right, dims, preferred_element_type=F32)


def three_products(left, right, dims, real_dot):
    half = left.shape[1] // 2
    left_re, left_im = left[:, :half], left[:, half:]
    right_re, right_im = right[:, :half], right[:, half:]
    first = real_dot(left_re, right_re, dims)
    second = real_dot(left_im, right_im, dims)
    if dims is NT:
        third = real_dot(left_re + left_im, right_re - right_im, dims)
        return jnp.concatenate([first + second, third - first + second], axis=1)
    third = real_dot(left_re + left_im, right_re + right_im, dims)
    return jnp.concatenate([first - second, third - first - second], axis=1)


def dot1(left, right, dims):
    return dot(left.astype(BF16), right.astype(BF16), dims)


def dot3(left, right, dims):
    left_hi, left_lo = split(left)
    right_hi, right_lo = split(right)
    return (dot(left_hi, right_hi, dims) + dot(left_lo, right_hi, dims)
            + dot(left_hi, right_lo, dims))


def mul1(left, right, dims=NN):
    return three_products(left, right, dims, dot1)


def mul3(left, right, dims=NN):
    return three_products(left, right, dims, dot3)


def adjoint(value):
    half = value.shape[1] // 2
    return jnp.concatenate([value[:, :half].T, -value[:, half:].T], axis=1)


def eye2(order):
    row = lax.broadcasted_iota(jnp.int32, (order, 2 * order), 0)
    col = lax.broadcasted_iota(jnp.int32, (order, 2 * order), 1)
    return jnp.where(row == col, 1.0, 0.0).astype(F32)


def total(value):
    return jnp.sum(value * value)


def invert(a_ref, ah_ref, pair_ref, floors):
    batch, order = a_ref.shape[:2]
    each = range(batch)
    bounds = []
    for j in each:
        normal = mul1(a_ref[j], a_ref[j], NT)
        bounds.append(jnp.sqrt(total(normal)))
        pair_ref[j, :order] = ah_ref[j] / bounds[j]
        pair_ref[j, order:] = normal / bounds[j]

    def rough(lows):
        after = []
        for j in each:
            low = lows[j]
            scale = 2.0 / (1.0 + low)
            pair = pair_ref[j]
            pair_ref[j] = (2.0 * scale) * pair - (scale * scale) * mul1(pair, pair[order:])
            rho = (1.0 - low) / (1.0 + low)
            after.append(1.0 - rho * rho)
        return tuple(after)

    lowest = lambda lows: functools.reduce(jnp.minimum, lows)
    largest = lambda sizes: functools.reduce(jnp.maximum, sizes)
    lax.while_loop(
        lambda lows: lowest(lows) < 0.9,
        rough,
        tuple(jnp.maximum(floors[j] / bounds[j], 1e-6) for j in each),
    )

    def newton(mul):
        def step(state):
            sizes = []
            for j in each:
                inverse = pair_ref[j, :order]
                left = eye2(order) - mul3(a_ref[j], inverse)
                pair_ref[j, :order] = inverse + mul(inverse, left)
                sizes.append(total(left))
            return state[0] + 1, largest(sizes)

        return step

    def iterate(mul, limit):
        return lax.while_loop(
            lambda s: (s[0] < limit) & (s[1] > 4e-6), newton(mul), (jnp.int32(0), F32(1.0))
        )[1]

    size = iterate(mul1, 5)

    @pl.when(jnp.logical_not(size <= 4e-6))
    def _():
        for j in each:
            pair_ref[j, :order] = ah_ref[j] / bounds[j]
        iterate(mul3, 60)


def green_kernel(scal_ref, side_ref, link_ref, far_ref, near_ref, sig_ref, green_ref, x_ref,
                 a_ref, ah_ref, pair_ref):
    order = far_ref.shape[-1]
    batch = sig_ref.shape[0]
    row = lax.broadcasted_iota(jnp.int32, (order, order), 0)
    col = lax.broadcasted_iota(jnp.int32, (order, order), 1)
    on = row == col

    def system(ham_ref, j, which):
        real = jnp.where(on, scal_ref[j] - sig_ref[j, which, 0:1, :], 0.0) - ham_ref[0]
        width = jnp.where(on, sig_ref[j, which, 1:2, :], 0.0)
        return (jnp.concatenate([real, width - ham_ref[1]], axis=1),
                jnp.concatenate([real, -width - ham_ref[1]], axis=1))

    def floors(which):
        least = [jnp.min(sig_ref[j, which, 1:2, :]) for j in range(batch)]
        return [value * value for value in least]

    for j in range(batch):
        a_ref[j], ah_ref[j] = system(far_ref, j, 1)
    invert(a_ref, ah_ref, pair_ref, floors(1))
    link = jnp.concatenate([link_ref[0], link_ref[1]], axis=1)
    link = jnp.where(side_ref[0] == 0, link, adjoint(link))
    for j in range(batch):
        x_ref[j] = mul3(link, pair_ref[j, :order])
        coupled = mul3(x_ref[j], link, NT)
        own, own_h = system(near_ref, j, 0)
        a_ref[j] = own - coupled
        ah_ref[j] = own_h - adjoint(coupled)
    invert(a_ref, ah_ref, pair_ref, floors(0))
    for j in range(batch):
        green_ref[j] = pair_ref[j, :order]


def lesser_greater(green, mixed, adj, near, far, g_rows, m_rows):
    order = green.shape[0]

    def source(sig):
        value = 2.0 * sig[2:3, :] * sig[1:2, :]
        return jnp.concatenate([value, value], axis=1)

    less = mul3(g_rows * source(near), green, NT) + mul3(m_rows * source(far), mixed, NT)
    k = jnp.concatenate([-less[:, order:], less[:, :order]], axis=1)
    return jnp.concatenate([k, k + g_rows - adj], axis=1)


def local_kernel(sig_ref, green_ref, x_ref, out_ref):
    green = green_ref[0]
    mixed = mul3(green, x_ref[0])
    out_ref[...] = lesser_greater(
        green, mixed, adjoint(green), sig_ref[0, 0], sig_ref[0, 1], green, mixed
    )


def exchange_kernel(sig_ref, green_ref, x_ref, out_ref, mix_ref, adj_ref, send_ref, recv_ref,
                    send_sem, recv_sem):
    peers, batch, rows = recv_ref.shape[:3]
    span = peers * rows
    order = green_ref.shape[1]
    spaces = lax.axis_size("space")
    per_side = peers // spaces
    where = lax.axis_index("energy")
    half = where // per_side
    me = (where - half * per_side) * spaces + lax.axis_index("space")

    def device(peer):
        return {"energy": half * per_side + peer // spaces, "space": peer % spaces}

    barrier = pltpu.get_barrier_semaphore()
    for hop in range(1, peers):
        pl.semaphore_signal(barrier, inc=1, device_id=device(me ^ hop),
                            device_id_type=pl.DeviceIdType.MESH)
    here = pl.ds(pl.multiple_of(half * span, span), span)
    copies = []
    for j in range(batch):
        mix_ref[...] = mul3(green_ref[j], x_ref[j])
        adj_ref[...] = adjoint(green_ref[j])
        send_ref[j] = lesser_greater(
            green_ref[j], mix_ref[...], adj_ref[here], sig_ref[j, 0], sig_ref[j, 1],
            green_ref[j, here], mix_ref[here],
        )
        if j == 0:
            pl.semaphore_wait(barrier, peers - 1)
        for hop in reversed(range(1, peers)):
            peer = me ^ hop
            copy = pltpu.make_async_remote_copy(
                src_ref=send_ref.at[j, pl.ds(pl.multiple_of(peer * rows, rows), rows)],
                dst_ref=recv_ref.at[me, j],
                send_sem=send_sem.at[j, hop],
                recv_sem=recv_sem.at[j, hop],
                device_id=device(peer),
                device_id_type=pl.DeviceIdType.MESH,
            )
            copy.start()
            copies.append(copy)
        recv_ref[me, j] = send_ref[j, pl.ds(pl.multiple_of(me * rows, rows), rows)]
    for copy in copies:
        copy.wait()
    count = per_side * batch
    for s in range(spaces):
        def part(n, i):
            return recv_ref[n % per_side * spaces + s, n // per_side, :, i * order:(i + 1) * order]

        for k in range(count):
            corr_re = jnp.zeros((rows, order), F32)
            corr_im = jnp.zeros((rows, order), F32)
            for n in range(k, count):
                kr, ki, qr, qi = part(n, 0), part(n, 1), part(n - k, 2), part(n - k, 3)
                corr_re += kr * qr + ki * qi
                corr_im += ki * qr - kr * qi
            out_ref[k, s, 0] = -order * corr_im
            out_ref[k, s, 1] = order * corr_re


VMEM = pl.BlockSpec(memory_space=pltpu.VMEM)
SMEM = pl.BlockSpec(memory_space=pltpu.SMEM)
LIMIT = 48 * 2**20


def green_blocks(energy, side, link, far, near, sig):
    order = far.shape[-1]
    batch = sig.shape[0]
    shape = (batch, order, 2 * order)
    return pl.pallas_call(
        green_kernel,
        out_shape=[jax.ShapeDtypeStruct(shape, F32)] * 2,
        in_specs=[SMEM, SMEM, VMEM, VMEM, VMEM, VMEM],
        out_specs=[VMEM, VMEM],
        scratch_shapes=[
            pltpu.VMEM(shape, F32),
            pltpu.VMEM(shape, F32),
            pltpu.VMEM((batch, 2 * order, 2 * order), F32),
        ],
        compiler_params=pltpu.CompilerParams(vmem_limit_bytes=LIMIT),
    )(energy, side, link, far, near, sig)


def exchange(sig, green, x, peers, rows):
    batch, order = green.shape[:2]
    spaces = lax.axis_size("space")
    return pl.pallas_call(
        exchange_kernel,
        out_shape=jax.ShapeDtypeStruct((peers // spaces * batch, spaces, 2, rows, order), F32),
        in_specs=[VMEM, VMEM, VMEM],
        out_specs=VMEM,
        scratch_shapes=[
            pltpu.VMEM((order, 2 * order), F32),
            pltpu.VMEM((order, 2 * order), F32),
            pltpu.VMEM((batch, peers * rows, 4 * order), F32),
            pltpu.VMEM((peers, batch, rows, 4 * order), F32),
            pltpu.SemaphoreType.DMA((batch, peers)),
            pltpu.SemaphoreType.DMA((batch, peers)),
        ],
        compiler_params=pltpu.CompilerParams(
            vmem_limit_bytes=LIMIT, collective_id=0, has_side_effects=True
        ),
    )(sig, green, x)


def collect(mine, count, sides, rows):
    order = mine.shape[0]
    arrived = lax.all_to_all(mine, ("energy", "space"), split_axis=0, concat_axis=0, tiled=True)
    arrived = arrived.reshape(count, sides, rows, 4, order)
    k_re, k_im, q_re, q_im = (arrived[:, :, :, i] for i in range(4))
    out = []
    for k in range(count):
        kr, ki = k_re[k:], k_im[k:]
        qr, qi = q_re[:count - k], q_im[:count - k]
        corr_re = jnp.sum(kr * qr + ki * qi, axis=0)
        corr_im = jnp.sum(ki * qr - kr * qi, axis=0)
        out.append(jnp.stack([-order * corr_im, order * corr_re], axis=1))
    return jnp.stack(out, axis=0)


SIDES = 2


def body(ham_diag, ham_coupling, sigma_shift, sigma_width, occupation):
    order = ham_diag.shape[-1]
    count = lax.axis_size("energy")
    spaces = lax.axis_size("space")
    side = lax.axis_index("space")
    where = lax.axis_index("energy")
    rows = order // (count * spaces)
    direct = rows % 8 == 0 and count & (count - 1) == 0
    batch = SIDES if direct and count % SIDES == 0 else 1
    per_side = count // batch
    near = ham_diag[0]
    far = lax.ppermute(near, "space", [(0, 1), (1, 0)])
    packed = jnp.concatenate([sigma_shift[0], sigma_width[0], occupation[0]], axis=0)
    sig = []
    for j in range(batch):
        pair = []
        for flip in range(spaces):
            moves = [(e * spaces + s, (e + j * per_side) % count * spaces + (s ^ flip))
                     for e in range(count) for s in range(spaces)]
            pair.append(packed if j == flip == 0 else lax.ppermute(packed, ("energy", "space"), moves))
        sig.append(jnp.stack(pair))
    index = (where + per_side * jnp.arange(batch)) % count
    energy = -2.0 + 4.0 * (index.astype(F32) + 0.5) / count
    sig = jnp.stack(sig)
    if batch > 1:
        flip = where >= per_side
        sig = jnp.where(flip, sig[::-1], sig)
        energy = jnp.where(flip, energy[::-1], energy)
    green, x = green_blocks(energy, side.reshape(1), ham_coupling[0], far, near, sig)
    if direct:
        return exchange(sig, green, x, per_side * spaces, rows)
    mine = pl.pallas_call(
        local_kernel,
        out_shape=jax.ShapeDtypeStruct((order, 4 * order), F32),
        in_specs=[VMEM, VMEM, VMEM],
        out_specs=VMEM,
        compiler_params=pltpu.CompilerParams(vmem_limit_bytes=LIMIT),
    )(sig, green, x)
    return collect(mine, count, spaces, rows)


def solution(mesh):
    return jax.shard_map(
        body,
        mesh=mesh,
        in_specs=(
            P("space", None, "groups", None),
            P("groups", None, None, None),
            P("energy", "space", "groups"),
            P("energy", "space", "groups"),
            P("energy", "space", "groups"),
        ),
        out_specs=P("groups", None, None, ("energy", "space"), None),
        check_vma=False,
    )
```

```python
import functools

import jax
import jax.numpy as jnp
from jax import lax
from jax.experimental import pallas as pl
from jax.experimental.pallas import tpu as pltpu
from jax.sharding import PartitionSpec as P

F32 = jnp.float32
BF16 = jnp.bfloat16
NN = (((1,), (0,)), ((), ()))
NT = (((1,), (1,)), ((), ()))


def split(value):
    high = value.astype(BF16)
    return high, (value - high.astype(F32)).astype(BF16)


def dot(left, right, dims):
    return lax.dot_general(left, right, dims, preferred_element_type=F32)


def three_products(left, right, dims, real_dot):
    half = left.shape[1] // 2
    left_re, left_im = left[:, :half], left[:, half:]
    right_re, right_im = right[:, :half], right[:, half:]
    first = real_dot(left_re, right_re, dims)
    second = real_dot(left_im, right_im, dims)
    if dims is NT:
        third = real_dot(left_re + left_im, right_re - right_im, dims)
        return jnp.concatenate([first + second, third - first + second], axis=1)
    third = real_dot(left_re + left_im, right_re + right_im, dims)
    return jnp.concatenate([first - second, third - first - second], axis=1)


def dot1(left, right, dims):
    return dot(left.astype(BF16), right.astype(BF16), dims)


def dot3(left, right, dims):
    left_hi, left_lo = split(left)
    right_hi, right_lo = split(right)
    return (dot(left_hi, right_hi, dims) + dot(left_lo, right_hi, dims)
            + dot(left_hi, right_lo, dims))


def mul1(left, right, dims=NN):
    return three_products(left, right, dims, dot1)


def mul3(left, right, dims=NN):
    return three_products(left, right, dims, dot3)


def adjoint(value):
    half = value.shape[1] // 2
    return jnp.concatenate([value[:, :half].T, -value[:, half:].T], axis=1)


def eye2(order):
    row = lax.broadcasted_iota(jnp.int32, (order, 2 * order), 0)
    col = lax.broadcasted_iota(jnp.int32, (order, 2 * order), 1)
    return jnp.where(row == col, 1.0, 0.0).astype(F32)


def total(value):
    return jnp.sum(value * value)


def invert(a_ref, ah_ref, pair_ref, floors):
    batch, order = a_ref.shape[:2]
    each = range(batch)
    bounds = []
    for j in each:
        normal = mul1(a_ref[j], a_ref[j], NT)
        mean = jnp.sum(normal * eye2(order)) / order
        spread = jnp.maximum(total(normal) / order - mean * mean, 0.0)
        bounds.append(1.02 * (mean + jnp.sqrt(spread * (order - 1.0))))
        pair_ref[j, :order] = ah_ref[j] / bounds[j]
        pair_ref[j, order:] = normal / bounds[j]

    def rough(lows):
        after = []
        for j in each:
            low = lows[j]
            scale = 2.0 / (1.0 + low)
            pair = pair_ref[j]
            pair_ref[j] = (2.0 * scale) * pair - (scale * scale) * mul1(pair, pair[order:])
            rho = (1.0 - low) / (1.0 + low)
            after.append(1.0 - rho * rho)
        return tuple(after)

    lowest = lambda lows: functools.reduce(jnp.minimum, lows)
    largest = lambda sizes: functools.reduce(jnp.maximum, sizes)
    lax.while_loop(
        lambda lows: lowest(lows) < 0.9,
        rough,
        tuple(jnp.maximum(floors[j] / bounds[j], 1e-6) for j in each),
    )

    def newton(mul):
        def step(state):
            sizes = []
            for j in each:
                inverse = pair_ref[j, :order]
                left = eye2(order) - mul3(a_ref[j], inverse)
                pair_ref[j, :order] = inverse + mul(inverse, left + mul(left, left))
                sizes.append(total(left))
            return state[0] + 1, largest(sizes)

        return step

    def iterate(mul, limit):
        return lax.while_loop(
            lambda s: (s[0] < limit) & (s[1] > 4e-4), newton(mul), (jnp.int32(0), F32(1.0))
        )[1]

    size = iterate(mul1, 5)

    @pl.when(jnp.logical_not(size <= 4e-4))
    def _():
        for j in each:
            pair_ref[j, :order] = ah_ref[j] / bounds[j]
        iterate(mul3, 60)


def green_kernel(scal_ref, side_ref, link_ref, far_ref, near_ref, sig_ref, green_ref, x_ref,
                 a_ref, ah_ref, pair_ref):
    order = far_ref.shape[-1]
    batch = sig_ref.shape[0]
    row = lax.broadcasted_iota(jnp.int32, (order, order), 0)
    col = lax.broadcasted_iota(jnp.int32, (order, order), 1)
    on = row == col

    def system(ham_ref, j, which):
        real = jnp.where(on, scal_ref[j] - sig_ref[j, which, 0:1, :], 0.0) - ham_ref[0]
        width = jnp.where(on, sig_ref[j, which, 1:2, :], 0.0)
        return (jnp.concatenate([real, width - ham_ref[1]], axis=1),
                jnp.concatenate([real, -width - ham_ref[1]], axis=1))

    def floors(which):
        least = [jnp.min(sig_ref[j, which, 1:2, :]) for j in range(batch)]
        return [value * value for value in least]

    for j in range(batch):
        a_ref[j], ah_ref[j] = system(far_ref, j, 1)
    invert(a_ref, ah_ref, pair_ref, floors(1))
    link = jnp.concatenate([link_ref[0], link_ref[1]], axis=1)
    link = jnp.where(side_ref[0] == 0, link, adjoint(link))
    for j in range(batch):
        x_ref[j] = mul3(link, pair_ref[j, :order])
        coupled = mul3(x_ref[j], link, NT)
        own, own_h = system(near_ref, j, 0)
        a_ref[j] = own - coupled
        ah_ref[j] = own_h - adjoint(coupled)
    invert(a_ref, ah_ref, pair_ref, floors(0))
    for j in range(batch):
        green_ref[j] = pair_ref[j, :order]


def lesser_greater(green, mixed, adj, near, far, g_rows, m_rows):
    order = green.shape[0]

    def source(sig):
        value = 2.0 * sig[2:3, :] * sig[1:2, :]
        return jnp.concatenate([value, value], axis=1)

    less = mul3(g_rows * source(near), green, NT) + mul3(m_rows * source(far), mixed, NT)
    k = jnp.concatenate([-less[:, order:], less[:, :order]], axis=1)
    return jnp.concatenate([k, k + g_rows - adj], axis=1)


def local_kernel(sig_ref, green_ref, x_ref, out_ref):
    green = green_ref[0]
    mixed = mul3(green, x_ref[0])
    out_ref[...] = lesser_greater(
        green, mixed, adjoint(green), sig_ref[0, 0], sig_ref[0, 1], green, mixed
    )


def exchange_kernel(sig_ref, green_ref, x_ref, out_ref, mix_ref, adj_ref, send_ref, recv_ref,
                    send_sem, recv_sem):
    peers, batch, rows = recv_ref.shape[:3]
    span = peers * rows
    order = green_ref.shape[1]
    spaces = lax.axis_size("space")
    per_side = peers // spaces
    where = lax.axis_index("energy")
    half = where // per_side
    me = (where - half * per_side) * spaces + lax.axis_index("space")

    def device(peer):
        return {"energy": half * per_side + peer // spaces, "space": peer % spaces}

    barrier = pltpu.get_barrier_semaphore()
    for hop in range(1, peers):
        pl.semaphore_signal(barrier, inc=1, device_id=device(me ^ hop),
                            device_id_type=pl.DeviceIdType.MESH)
    here = pl.ds(pl.multiple_of(half * span, span), span)
    copies = []
    for j in range(batch):
        mix_ref[...] = mul3(green_ref[j], x_ref[j])
        adj_ref[...] = adjoint(green_ref[j])
        send_ref[j] = lesser_greater(
            green_ref[j], mix_ref[...], adj_ref[here], sig_ref[j, 0], sig_ref[j, 1],
            green_ref[j, here], mix_ref[here],
        )
        if j == 0:
            pl.semaphore_wait(barrier, peers - 1)
        for hop in reversed(range(1, peers)):
            peer = me ^ hop
            copy = pltpu.make_async_remote_copy(
                src_ref=send_ref.at[j, pl.ds(pl.multiple_of(peer * rows, rows), rows)],
                dst_ref=recv_ref.at[me, j],
                send_sem=send_sem.at[j, hop],
                recv_sem=recv_sem.at[j, hop],
                device_id=device(peer),
                device_id_type=pl.DeviceIdType.MESH,
            )
            copy.start()
            copies.append(copy)
        recv_ref[me, j] = send_ref[j, pl.ds(pl.multiple_of(me * rows, rows), rows)]
    for copy in copies:
        copy.wait()
    count = per_side * batch
    for s in range(spaces):
        def part(n, i):
            return recv_ref[n % per_side * spaces + s, n // per_side, :, i * order:(i + 1) * order]

        for k in range(count):
            corr_re = jnp.zeros((rows, order), F32)
            corr_im = jnp.zeros((rows, order), F32)
            for n in range(k, count):
                kr, ki, qr, qi = part(n, 0), part(n, 1), part(n - k, 2), part(n - k, 3)
                corr_re += kr * qr + ki * qi
                corr_im += ki * qr - kr * qi
            out_ref[k, s, 0] = -order * corr_im
            out_ref[k, s, 1] = order * corr_re


VMEM = pl.BlockSpec(memory_space=pltpu.VMEM)
SMEM = pl.BlockSpec(memory_space=pltpu.SMEM)
LIMIT = 48 * 2**20


def green_blocks(energy, side, link, far, near, sig):
    order = far.shape[-1]
    batch = sig.shape[0]
    shape = (batch, order, 2 * order)
    return pl.pallas_call(
        green_kernel,
        out_shape=[jax.ShapeDtypeStruct(shape, F32)] * 2,
        in_specs=[SMEM, SMEM, VMEM, VMEM, VMEM, VMEM],
        out_specs=[VMEM, VMEM],
        scratch_shapes=[
            pltpu.VMEM(shape, F32),
            pltpu.VMEM(shape, F32),
            pltpu.VMEM((batch, 2 * order, 2 * order), F32),
        ],
        compiler_params=pltpu.CompilerParams(vmem_limit_bytes=LIMIT),
    )(energy, side, link, far, near, sig)


def exchange(sig, green, x, peers, rows):
    batch, order = green.shape[:2]
    spaces = lax.axis_size("space")
    return pl.pallas_call(
        exchange_kernel,
        out_shape=jax.ShapeDtypeStruct((peers // spaces * batch, spaces, 2, rows, order), F32),
        in_specs=[VMEM, VMEM, VMEM],
        out_specs=VMEM,
        scratch_shapes=[
            pltpu.VMEM((order, 2 * order), F32),
            pltpu.VMEM((order, 2 * order), F32),
            pltpu.VMEM((batch, peers * rows, 4 * order), F32),
            pltpu.VMEM((peers, batch, rows, 4 * order), F32),
            pltpu.SemaphoreType.DMA((batch, peers)),
            pltpu.SemaphoreType.DMA((batch, peers)),
        ],
        compiler_params=pltpu.CompilerParams(
            vmem_limit_bytes=LIMIT, collective_id=0, has_side_effects=True
        ),
    )(sig, green, x)


def collect(mine, count, sides, rows):
    order = mine.shape[0]
    arrived = lax.all_to_all(mine, ("energy", "space"), split_axis=0, concat_axis=0, tiled=True)
    arrived = arrived.reshape(count, sides, rows, 4, order)
    k_re, k_im, q_re, q_im = (arrived[:, :, :, i] for i in range(4))
    out = []
    for k in range(count):
        kr, ki = k_re[k:], k_im[k:]
        qr, qi = q_re[:count - k], q_im[:count - k]
        corr_re = jnp.sum(kr * qr + ki * qi, axis=0)
        corr_im = jnp.sum(ki * qr - kr * qi, axis=0)
        out.append(jnp.stack([-order * corr_im, order * corr_re], axis=1))
    return jnp.stack(out, axis=0)


SIDES = 2


def body(ham_diag, ham_coupling, sigma_shift, sigma_width, occupation):
    order = ham_diag.shape[-1]
    count = lax.axis_size("energy")
    spaces = lax.axis_size("space")
    side = lax.axis_index("space")
    where = lax.axis_index("energy")
    rows = order // (count * spaces)
    direct = rows % 8 == 0 and count & (count - 1) == 0
    batch = SIDES if direct and count % SIDES == 0 else 1
    per_side = count // batch
    near = ham_diag[0]
    far = lax.ppermute(near, "space", [(0, 1), (1, 0)])
    packed = jnp.concatenate([sigma_shift[0], sigma_width[0], occupation[0]], axis=0)
    sig = []
    for j in range(batch):
        pair = []
        for flip in range(spaces):
            moves = [(e * spaces + s, (e + j * per_side) % count * spaces + (s ^ flip))
                     for e in range(count) for s in range(spaces)]
            pair.append(packed if j == flip == 0 else lax.ppermute(packed, ("energy", "space"), moves))
        sig.append(jnp.stack(pair))
    index = (where + per_side * jnp.arange(batch)) % count
    energy = -2.0 + 4.0 * (index.astype(F32) + 0.5) / count
    sig = jnp.stack(sig)
    if batch > 1:
        flip = where >= per_side
        sig = jnp.where(flip, sig[::-1], sig)
        energy = jnp.where(flip, energy[::-1], energy)
    green, x = green_blocks(energy, side.reshape(1), ham_coupling[0], far, near, sig)
    if direct:
        return exchange(sig, green, x, per_side * spaces, rows)
    mine = pl.pallas_call(
        local_kernel,
        out_shape=jax.ShapeDtypeStruct((order, 4 * order), F32),
        in_specs=[VMEM, VMEM, VMEM],
        out_specs=VMEM,
        compiler_params=pltpu.CompilerParams(vmem_limit_bytes=LIMIT),
    )(sig, green, x)
    return collect(mine, count, spaces, rows)


def solution(mesh):
    return jax.shard_map(
        body,
        mesh=mesh,
        in_specs=(
            P("space", None, "groups", None),
            P("groups", None, None, None),
            P("energy", "space", "groups"),
            P("energy", "space", "groups"),
            P("energy", "space", "groups"),
        ),
        out_specs=P("groups", None, None, ("energy", "space"), None),
        check_vma=False,
    )
```
